32 devices in a mesh: parts: 2 (over y), dp: 4 (over z), tensor: 4 (over x, core).
Axes of the slice: x: 2, y: 2, z: 4, core: 2. Of those that a mesh axis runs over, the one named last changes fastest.
Arguments:
- queries: bfloat16 [6144, 6144], P(('parts', 'dp'), 'tensor'), parts along dimension 0, may hold values from -6 to 6
- keys: bfloat16 [6144, 6144], P(('parts', 'dp'), 'tensor'), parts along dimension 0, may hold values from -8 to 8
- values: bfloat16 [6144, 6144], P(('parts', 'dp'), 'tensor'), parts along dimension 0, may hold values from -6 to 6
- segment: int32 [6144], P(('parts', 'dp')), parts along dimension 0, may hold values from 0 to 23, as said below
- w_out: bfloat16 [6144, 5120], P('tensor'), may hold values from -0.109375 to 0.109375
- w_scale: float32 [48, 40], P('tensor'), may hold values from 0.25 to 4
- handover: int32 [6], P('parts'), parts along dimension 0, may hold values from 0 to 3, as said below
Outputs:
- handed: bfloat16 [5120, 6144], P('tensor', ('parts', 'dp')), parts along dimension 1
The draws below stay inside these ranges and needn't reach their ends.
There are 2 independent parts, one for each index of `parts`. The reference program is written for one: setup_inputs(seed, part) draws one part's arguments, and reference() takes and returns one part's arrays. A program takes and returns all parts, laid end to end along the dimension named above; an argument that names none is the same for every part. Nothing has to cross between parts.
Inputs may be any that keep to these rules, and one draw needn't show every extreme that they name: Within each group's 768 rows the segment numbers start at 0, never fall and rise by at most one from row to row; a new sequence starts only at a multiple of 32 rows, and always at each multiple of 256 rows past the first. `handover`: every distance appears at most 1 times, and some distance exactly 1 times.
All inputs are finite; a program needn't handle non-finite values.
Results may differ from the reference program's by a relative error of at most 0.0095.
Values may be sent and summed in bfloat16 or wider, within the bound.
No kernel may reach another device: no remote copies, remote signals or barrier semaphores. Data moves between devices by JAX's collectives and lax.ppermute only.
A program may use at most 192 MiB of HBM per device.

```python
import math
import jax
import jax.numpy as jnp
from jax import lax

D = 5120
HEADS = 48
HD = 128
QB = 128
SPAN = 32
PIECE = 256
ROWS_DEV = 768
ROWS = 3072
PIECES = 3
N_DP = 4
N_TENSOR = 4


def draw_queries(key, part):
    key = jax.random.fold_in(key, 11)
    base = jax.random.normal(key, (ROWS, HEADS * HD), jnp.float32)
    return jnp.clip(base, -6.0, 6.0).astype(jnp.bfloat16)


def draw_keys(key, part):
    key = jax.random.fold_in(key, 12)
    noise_key, scale_key = jax.random.split(key)
    row_scale = jnp.exp(jax.random.uniform(scale_key, (ROWS, 1), jnp.float32, jnp.log(0.3), jnp.log(3.0)))
    base = jax.random.normal(noise_key, (ROWS, HEADS * HD), jnp.float32) * row_scale
    return jnp.clip(base, -8.0, 8.0).astype(jnp.bfloat16)


def draw_segment(key, part):
    key = jax.random.fold_in(key, 21)
    level_key, roll_key, pick_key = jax.random.split(key, 3)
    group_count = ROWS // ROWS_DEV
    level = jax.random.randint(level_key, (group_count, 1), 2, 5)
    chosen = jax.random.randint(pick_key, (), 0, group_count)
    level = jnp.where(jnp.arange(group_count)[:, None] == chosen, 0, level)
    rolled = jax.random.randint(roll_key, (group_count, ROWS_DEV), 0, 4)
    position = jnp.arange(ROWS_DEV)[None, :]
    boundary = (position % PIECE == 0) & (position > 0)
    starting = boundary | (position % SPAN == 0) & (position > 0) & (rolled < level)
    return jnp.cumsum(starting.astype(jnp.int32), axis=1).reshape(ROWS).astype(jnp.int32)


def draw_handover(key, part):
    key = jax.random.fold_in(key, 31)
    group_count = ROWS // ROWS_DEV
    ordering = jax.random.permutation(key, group_count)
    return ordering[jnp.arange(PIECES) % group_count].astype(jnp.int32)


def spiked(values, key, source, target, parts, factor):
    owner, partner = [(jnp.arange(values.shape[dim]) // (values.shape[dim] // parts)).reshape([-1 if axis == dim else 1 for axis in range(values.ndim)]) for dim in (source, target)]
    chosen = jax.random.permutation(key, parts)[partner]
    strong = (owner == chosen) | (owner == (partner + parts // 2) % parts)
    return jnp.where(strong, factor * values, values)


def block_levels(rng, extent, cuts, smallest, largest):
    factor_of, own = 1.0, jax.random.fold_in(rng, 6)
    for dim, blocks in cuts:
        heights = jnp.exp(jax.random.uniform(jax.random.fold_in(own, dim), (blocks,), jnp.float32, smallest / len(cuts), largest / len(cuts)))
        factor_of = factor_of * jnp.repeat(heights, extent[dim] // blocks).reshape([-1 if axis == dim else 1 for axis in range(len(extent))])
    return factor_of


def gaussian(rng, extent, deviation, bound, cuts=(), held_as=jnp.bfloat16):
    result = deviation * jax.random.normal(rng, extent, jnp.float32)
    if cuts:
        result = result * block_levels(rng, extent, cuts, -0.22, 0.18)
    return jnp.clip(result, -bound, bound).astype(held_as)


def heavy_noise(own_key, dims, scale, limit, shards, heavy, kind=jnp.bfloat16):
    entries = scale * jax.random.normal(own_key, dims, jnp.float32)
    if shards:
        entries = entries * block_levels(own_key, dims, shards, -0.22, 0.18)
    return jnp.clip(spiked(entries, jax.random.fold_in(own_key, 3), *heavy), -limit, limit).astype(kind)


def setup_inputs(seed: int = 0, part: int = 0) -> dict:
    splits = jax.random.split(jax.random.key(seed), 8)
    part_keys = jax.random.split(jax.random.fold_in(splits[7], part), 8)
    queries = draw_queries(jax.random.fold_in(jax.random.fold_in(splits[7], part), 71), part)
    keys = draw_keys(jax.random.fold_in(jax.random.fold_in(splits[7], part), 71), part)
    values = gaussian(part_keys[2], (ROWS, HEADS * HD), 1.0, 6.0, ((0, 4), (1, 4)))
    segment = draw_segment(jax.random.fold_in(jax.random.fold_in(splits[7], part), 71), part)
    w_out = heavy_noise(splits[4], (HEADS * HD, D), (HEADS * HD) ** -0.5, 0.109375, ((0, 4),), (0, 1, 4, 2.0))
    w_scale = jnp.clip(jnp.exp(math.log(4.0) - 2.7725887 * jax.random.uniform(splits[5], (HEADS * HD // QB, D // QB), jnp.float32) ** block_levels(splits[5], (HEADS * HD // QB, D // QB), ((0, 4),), -0.2, 0.2)), 0.25, 4.0)
    handover = draw_handover(jax.random.fold_in(jax.random.fold_in(splits[7], part), 71), part)
    return dict(queries=queries, keys=keys, values=values, segment=segment, w_out=w_out, w_scale=w_scale, handover=handover)


NEG = -1.0e30


def group_attention(block):
    group_queries, group_keys, group_values, group_segment = block
    row_count = group_queries.shape[0]
    q_heads = group_queries.reshape(row_count, HEADS, HD).astype(jnp.float32)
    k_heads = group_keys.reshape(row_count, HEADS, HD).astype(jnp.float32)
    v_heads = group_values.reshape(row_count, HEADS, HD).astype(jnp.float32)
    scores = jnp.einsum("qhd,khd->hqk", q_heads, k_heads) * (HD ** -0.5)
    allowed = (group_segment[:, None] == group_segment[None, :])[None]
    row_top = jnp.max(jnp.where(allowed, scores, NEG), axis=2, keepdims=True)
    weights = jnp.where(allowed, jnp.exp(scores - row_top), 0.0)
    row_total = jnp.sum(weights, axis=2)
    rounded = lax.optimization_barrier(weights.astype(jnp.bfloat16)).astype(jnp.float32)
    blended = jnp.einsum("hqk,khd->qhd", rounded, v_heads)
    blended = blended / jnp.transpose(row_total)[:, :, None]
    return blended.reshape(row_count, HEADS * HD).astype(jnp.bfloat16)


def dequantize(w_out, w_scale):
    scale_rows, scale_cols = w_scale.shape
    total_rows, total_cols = w_out.shape
    blocked = w_out.astype(jnp.float32).reshape(scale_rows, total_rows // scale_rows, scale_cols, total_cols // scale_cols)
    blocked = blocked * w_scale[:, None, :, None]
    return blocked.reshape(total_rows, total_cols).astype(jnp.bfloat16)


def reference(queries, keys, values, segment, w_out, w_scale, handover):
    grouped = (queries.reshape(N_DP, ROWS_DEV, HEADS * HD), keys.reshape(N_DP, ROWS_DEV, HEADS * HD),
               values.reshape(N_DP, ROWS_DEV, HEADS * HD), segment.reshape(N_DP, ROWS_DEV))
    attended = lax.map(group_attention, grouped).reshape(ROWS, HEADS * HD)
    weight = dequantize(w_out, w_scale)
    width = HEADS * HD // N_TENSOR

    def add_group(summed, group_index):
        columns = lax.dynamic_slice_in_dim(attended, (group_index * width).astype(jnp.int32), width, 1)
        rows_part = lax.dynamic_slice_in_dim(weight, (group_index * width).astype(jnp.int32), width, 0)
        partial_value = jnp.dot(columns, rows_part, preferred_element_type=jnp.float32)
        partial_value = lax.optimization_barrier(partial_value.astype(jnp.bfloat16)).astype(jnp.float32)
        return summed + jnp.transpose(partial_value), None

    summed, _ = lax.scan(add_group, jnp.zeros((D, ROWS), jnp.float32), jnp.arange(N_TENSOR, dtype=jnp.int32))
    home = summed.astype(jnp.bfloat16)
    pieces = home.reshape(D, N_DP, PIECES, PIECE)
    source = jnp.mod(jnp.arange(N_DP, dtype=jnp.int32)[:, None] - handover[None, :], N_DP).astype(jnp.int32)
    slot = jnp.arange(PIECES, dtype=jnp.int32)[None, :]
    handed = pieces[:, source, slot, :]
    return handed.reshape(D, ROWS)
```

```python
import functools

import jax
import jax.numpy as jnp
from jax import lax
from jax.experimental import pallas as pl
from jax.experimental.pallas import tpu as pltpu
from jax.sharding import PartitionSpec as P

HD = 128
PIECE = 256
WIDE = 256
NEG = -1e30
LOG2E = 1.4426950408889634
VMEM = 28 * 1024 * 1024
HEADS_STEP = 4

ANY = pl.BlockSpec(memory_space=pl.ANY)


def params():
    return pltpu.CompilerParams(vmem_limit_bytes=VMEM)


def attend_heads(heads, q_ref, k_ref, v_ref, bias, o_ref, first=0):
    ones = jnp.ones((PIECE, HD), jnp.bfloat16)
    for h in range(first, first + heads):
        cols = slice(h * HD, (h + 1) * HD)
        scores = lax.dot_general(
            q_ref[:, cols], k_ref[:, cols], (((1,), (1,)), ((), ())), preferred_element_type=jnp.float32
        )
        scores = scores * (LOG2E * HD ** -0.5) + bias
        top = jnp.max(scores, axis=1, keepdims=True)
        weights = jnp.exp2(scores - top).astype(jnp.bfloat16)
        both = jnp.concatenate([v_ref[:, cols], ones], axis=1)
        mixed = jnp.dot(weights, both, preferred_element_type=jnp.float32)
        o_ref[:, cols] = (mixed[:, :HD] / mixed[:, HD:]).astype(jnp.bfloat16)


def segment_bias(numbers):
    across = jnp.broadcast_to(numbers.astype(jnp.float32), (PIECE, PIECE))
    return jnp.where(across == jnp.transpose(across), 0.0, NEG)


def piece_at(meta_ref, distance):
    piece = jnp.where(meta_ref[1] == distance, 0, jnp.where(meta_ref[2] == distance, 1, 2))
    return pl.multiple_of(piece * PIECE, PIECE)


def scaled_product(a_ref, w_ref, s_ref, local_col, global_col):
    rows = []
    for kb in range(w_ref.shape[0] // HD):
        blocks = []
        for fb in range(WIDE // HD):
            tile = w_ref[kb * HD:(kb + 1) * HD, local_col + fb * HD:local_col + (fb + 1) * HD]
            scale = s_ref[kb, global_col // HD + fb]
            blocks.append((tile.astype(jnp.float32) * scale).astype(jnp.bfloat16))
        rows.append(jnp.concatenate(blocks, axis=1))
    return jnp.dot(a_ref[...], jnp.concatenate(rows, axis=0), preferred_element_type=jnp.float32)


def spans(me, features, flip, ranges):
    away, home = (me ^ 2) ^ flip, me ^ flip
    return [
        (pl.multiple_of(rank * features + first, HD), width) for rank in (away, home) for first, width in ranges
    ]


def sibling_kernel(features, distance, ranges, attend, meta_ref, *refs):
    if attend:
        q_hbm, k_hbm, v_hbm, seg_hbm, w_hbm, s_hbm, _, o_hbm, att_hbm = refs[:9]
        att, w_ref, s_ref, out, w_sem, o_sem, s_sem, q_ref, k_ref, v_ref, seg_ref, in_sem, seg_sem, att_sem = refs[9:]
        first_row = piece_at(meta_ref, distance)
        groups = q_ref.shape[1] // (HEADS_STEP * HD)
        loads = []
        seg_load = pltpu.make_async_copy(seg_hbm.at[pl.ds(first_row // PIECE, 1)], seg_ref, seg_sem)
        seg_load.start()
        for g in range(groups):
            cols = pl.ds(g * HEADS_STEP * HD, HEADS_STEP * HD)
            for i, (source, dest) in enumerate(((q_hbm, q_ref), (k_hbm, k_ref), (v_hbm, v_ref))):
                load = pltpu.make_async_copy(
                    source.at[pl.ds(first_row, PIECE), cols], dest.at[:, cols], in_sem.at[g, i]
                )
                load.start()
                loads.append(load)
    else:
        att_hbm, w_hbm, s_hbm, _, o_hbm = refs[:5]
        att, w_ref, s_ref, out, w_sem, o_sem, s_sem, att_sem = refs[5:]
        att_load = pltpu.make_async_copy(att_hbm, att, att_sem)
        att_load.start()
    scale_load = pltpu.make_async_copy(s_hbm, s_ref, s_sem)
    scale_load.start()
    columns = spans(meta_ref[0], features, 1, ranges)
    w_loads, at = [], 0
    for i, (first, width) in enumerate(columns):
        load = pltpu.make_async_copy(w_hbm.at[:, pl.ds(first, width)], w_ref.at[:, pl.ds(at, width)], w_sem.at[i])
        load.start()
        w_loads.append(load)
        at += width
    if attend:
        seg_load.wait()
        bias = segment_bias(seg_ref[0])
        for g in range(groups):
            for load in loads[3 * g:3 * g + 3]:
                load.wait()
            attend_heads(HEADS_STEP, q_ref, k_ref, v_ref, bias, att, g * HEADS_STEP)
        att_store = pltpu.make_async_copy(att, att_hbm, att_sem)
        att_store.start()
    else:
        att_load.wait()
    scale_load.wait()
    stores, at = [], 0
    for i, (first, width) in enumerate(columns):
        w_loads[i].wait()
        for inner in range(0, width, WIDE):
            product = scaled_product(att, w_ref, s_ref, at + inner, first + inner)
            out[:, at + inner:at + inner + WIDE] = product.astype(jnp.bfloat16)
        store = pltpu.make_async_copy(out.at[:, pl.ds(at, width)], o_hbm.at[:, pl.ds(at, width)], o_sem.at[i])
        store.start()
        stores.append(store)
        at += width
    for store in stores:
        store.wait()
    if attend:
        att_store.wait()


def sibling_part(meta, distance, ranges, inputs, attended, w_out, w_scale, features, token):
    rows, depth = PIECE, w_out.shape[0]
    total = 2 * sum(width for _, width in ranges)
    attend = attended is None
    bf16 = jnp.bfloat16
    scratch = [
        pltpu.VMEM((rows, depth), bf16),
        pltpu.VMEM((depth, total), bf16),
        pltpu.SMEM(w_scale.shape, jnp.float32),
        pltpu.VMEM((rows, total), bf16),
        pltpu.SemaphoreType.DMA((2 * len(ranges),)),
        pltpu.SemaphoreType.DMA((2 * len(ranges),)),
        pltpu.SemaphoreType.DMA,
    ]
    shapes = [jax.ShapeDtypeStruct((rows, total), bf16)]
    if attend:
        scratch += [pltpu.VMEM((rows, depth), bf16)] * 3
        scratch += [pltpu.VMEM((1, 1, PIECE), jnp.int32)]
        scratch += [pltpu.SemaphoreType.DMA((depth // (HEADS_STEP * HD), 3)), pltpu.SemaphoreType.DMA]
        shapes.append(jax.ShapeDtypeStruct((rows, depth), bf16))
    operands = (tuple(inputs) if attend else (attended,)) + (w_out, w_scale, token)
    return pl.pallas_call(
        functools.partial(sibling_kernel, features, distance, ranges, attend),
        grid_spec=pltpu.PrefetchScalarGridSpec(
            num_scalar_prefetch=1,
            grid=(1,),
            in_specs=[ANY] * len(operands),
            out_specs=[ANY] * len(shapes),
            scratch_shapes=scratch + [pltpu.SemaphoreType.DMA],
        ),
        out_shape=shapes,
        compiler_params=params(),
        cost_estimate=COST,
    )(meta, *operands)


def own_kernel(features, chunk, at, stride, meta_ref, att_hbm, w_hbm, s_hbm, r_hbm, _, send_hbm, keep_hbm, *scratch):
    att, w_ref, s_ref, r_ref, out, w_sem, r_sem, o_sem, s_sem, att_sem = scratch
    width = chunk[1]
    att_load = pltpu.make_async_copy(att_hbm, att, att_sem)
    att_load.start()
    scale_load = pltpu.make_async_copy(s_hbm, s_ref, s_sem)
    scale_load.start()
    columns = spans(meta_ref[0], features, 0, [chunk])
    loads = []
    for i, (first, _) in enumerate(columns):
        load = pltpu.make_async_copy(
            w_hbm.at[:, pl.ds(first, width)], w_ref.at[:, pl.ds(i * width, width)], w_sem.at[i]
        )
        load.start()
        received = pltpu.make_async_copy(
            r_hbm.at[:, pl.ds(i * stride + at, width)], r_ref.at[:, pl.ds(i * width, width)], r_sem.at[i]
        )
        received.start()
        loads.append((load, received))
    att_load.wait()
    scale_load.wait()
    stores = []
    for i, (first, _) in enumerate(columns):
        for load in loads[i]:
            load.wait()
        for inner in range(0, width, WIDE):
            cols = slice(i * width + inner, i * width + inner + WIDE)
            product = scaled_product(att, w_ref, s_ref, i * width + inner, first + inner)
            out[:, cols] = (product + r_ref[:, cols].astype(jnp.float32)).astype(jnp.bfloat16)
        store = pltpu.make_async_copy(out.at[:, pl.ds(i * width, width)], (send_hbm, keep_hbm)[i], o_sem.at[i])
        store.start()
        stores.append(store)
    for store in stores:
        store.wait()


def own_part(meta, chunk, at, stride, attended, w_out, w_scale, received, features, token):
    rows, depth = attended.shape
    width = chunk[1]
    bf16 = jnp.bfloat16
    return pl.pallas_call(
        functools.partial(own_kernel, features, chunk, at, stride),
        grid_spec=pltpu.PrefetchScalarGridSpec(
            num_scalar_prefetch=1,
            grid=(1,),
            in_specs=[ANY] * 5,
            out_specs=[ANY] * 2,
            scratch_shapes=[
                pltpu.VMEM((rows, depth), bf16),
                pltpu.VMEM((depth, 2 * width), bf16),
                pltpu.SMEM(w_scale.shape, jnp.float32),
                pltpu.VMEM((rows, 2 * width), bf16),
                pltpu.VMEM((rows, 2 * width), bf16),
                pltpu.SemaphoreType.DMA((2,)),
                pltpu.SemaphoreType.DMA((2,)),
                pltpu.SemaphoreType.DMA((2,)),
                pltpu.SemaphoreType.DMA,
                pltpu.SemaphoreType.DMA,
            ],
        ),
        out_shape=[jax.ShapeDtypeStruct((rows, width), bf16)] * 2,
        compiler_params=params(),
        cost_estimate=COST,
    )(meta, attended, w_out, w_scale, received, token)


def finish_kernel(distance, first, sums, into, settles, meta_ref, *refs):
    refs = list(refs)
    whole = refs.pop(-3) if into else None
    out, sem = refs[-2:]
    inputs = 2 if sums else 0
    stores = []
    for i, (far, at) in enumerate(settles):
        source = refs[inputs + i]
        dest = whole.at[pl.ds(at, source.shape[0]), pl.ds(piece_at(meta_ref, far), PIECE)]
        stores.append(pltpu.make_async_copy(source, dest, sem.at[1 + i]))
    for store in stores:
        store.start()
    if sums:
        keep_ref, r_ref = refs[:2]
        width = keep_ref.shape[1]
        for at in range(0, width, WIDE):
            cols = slice(at, at + WIDE)
            total = keep_ref[:, cols].astype(jnp.float32) + r_ref[:, cols].astype(jnp.float32)
            out[cols, :] = jnp.transpose(total.astype(jnp.bfloat16))
        if distance:
            dest = refs[-3]
        else:
            dest = whole.at[pl.ds(first, width), pl.ds(piece_at(meta_ref, distance), PIECE)]
        store = pltpu.make_async_copy(out, dest, sem.at[0])
        store.start()
        stores.append(store)
    for store in stores:
        store.wait()


def finish(meta, distance, first, pair, arrivals, whole, target, token):
    into = bool(arrivals) or (bool(pair) and distance == 0)
    arrays = list(pair) + [chunk for _, _, chunk in arrivals]
    specs = [pl.BlockSpec(array.shape, lambda g, meta: (0, 0)) for array in arrays]
    if token is not whole:
        arrays, specs = arrays + [token], specs + [ANY]
    shapes, aliases = [], {}
    scratch_shape = (pair[0].shape[1], PIECE) if pair else (16, HD)
    if pair and distance:
        shapes.append(jax.ShapeDtypeStruct(scratch_shape, jnp.bfloat16))
    if into:
        if whole is not None:
            aliases = {1 + len(arrays): len(shapes)}
            arrays, specs = arrays + [whole], specs + [ANY]
        shapes.append(target)
    result = pl.pallas_call(
        functools.partial(finish_kernel, distance, first, bool(pair), into, [a[:2] for a in arrivals]),
        grid_spec=pltpu.PrefetchScalarGridSpec(
            num_scalar_prefetch=1,
            grid=(1,),
            in_specs=specs,
            out_specs=[ANY] * len(shapes),
            scratch_shapes=[
                pltpu.VMEM(scratch_shape, jnp.bfloat16), pltpu.SemaphoreType.DMA((1 + len(arrivals),))
            ],
        ),
        out_shape=shapes,
        input_output_aliases=aliases,
        compiler_params=params(),
        cost_estimate=COST,
    )(meta, *arrays)
    return (result[0] if pair and distance else None), (result[-1] if into else whole)


COST = pl.CostEstimate(flops=1000, bytes_accessed=1000, transcendentals=0)


CHUNKS = ((0, 0, 256), (0, 256, 512), (0, 768, 512), (1, 0, 768), (1, 768, 512), (2, 0, 1280))
SHARES = ((0, ((0, 256),)), (0, ((256, 512), (768, 512))), (1, ((0, 768), (768, 512))), (2, ((0, 768), (768, 512))))
STEPS = (
    ("share", 0), ("own", 0), ("share", 1), ("finish", 0, ()), ("own", 1), ("share", 2), ("own", 2), ("finish", 1, (0,)),
    ("own", 3), ("finish", 2, ()), ("own", 4), ("share", 3), ("finish", 3, (1,)), ("own", 5), ("finish", 4, (2,)),
    ("finish", 5, (3,)), ("finish", None, (4,)), ("finish", None, (5,)),
)


def pipeline(distances, meta, queries, keys, values, segment, w_out, w_scale):
    groups = lax.axis_size("dp")
    ranks = lax.axis_size("tensor")
    features = w_out.shape[1] // ranks
    other_core = [(i, i ^ 1) for i in range(ranks)]
    other_chip = [(i, i ^ 2) for i in range(ranks)]
    target = jax.ShapeDtypeStruct((features, queries.shape[0]), jnp.bfloat16)
    attended, from_core, kept, from_chip, arrived = {}, {}, {}, {}, {}
    token, whole = meta, None
    for step, index, *rest in STEPS:
        if step == "share":
            piece, ranges = SHARES[index]
            result = sibling_part(
                meta, distances[piece], ranges, (queries, keys, values, segment), attended.get(piece), w_out, w_scale,
                features, token,
            )
            if len(result) == 2:
                attended[piece] = result[1]
            token = result[0]
            share, at = lax.ppermute(token, "tensor", other_core), 0
            for first, width in ranges:
                from_core[piece, first] = (share, at, sum(w for _, w in ranges))
                at += width
        elif step == "own":
            piece, first, width = CHUNKS[index]
            share, at, stride = from_core[piece, first]
            send, kept[index] = own_part(
                meta, (first, width), at, stride, attended[piece], w_out, w_scale, share, features, token
            )
            token = kept[index]
            from_chip[index] = lax.ppermute(send, "tensor", other_chip)
        else:
            settled = [i for i in rest[0] if i in arrived]
            if index is None and not settled:
                continue
            piece, first, _ = CHUNKS[index] if index is not None else (0, 0, 0)
            distance = distances[piece]
            chunk, whole = finish(
                meta,
                distance,
                first,
                () if index is None else (kept[index], from_chip[index]),
                [(distances[CHUNKS[i][0]], CHUNKS[i][1], arrived[i]) for i in settled],
                whole,
                target,
                token,
            )
            token = whole if chunk is None else chunk
            if chunk is not None:
                shift = [(i, (i + distance) % groups) for i in range(groups)]
                arrived[index] = lax.ppermute(chunk, "dp", shift)
    return whole


def attention_kernel(heads, q_ref, k_ref, v_ref, seg_ref, o_ref):
    attend_heads(heads, q_ref, k_ref, v_ref, segment_bias(seg_ref[0]), o_ref)


def attend_all(queries, keys, values, segment):
    rows, width = queries.shape
    heads = HEADS_STEP if (width // HD) % HEADS_STEP == 0 else 1
    block = pl.BlockSpec((PIECE, heads * HD), lambda i, g: (i, g))
    return pl.pallas_call(
        functools.partial(attention_kernel, heads),
        grid=(rows // PIECE, width // (heads * HD)),
        in_specs=[block, block, block, pl.BlockSpec((1, 1, PIECE), lambda i, g: (i, 0, 0))],
        out_specs=block,
        out_shape=jax.ShapeDtypeStruct((rows, width), jnp.bfloat16),
        compiler_params=params(),
    )(queries, keys, values, segment)


def general(queries, keys, values, segment, w_out, w_scale, handover):
    row_count, width = queries.shape
    piece_count = handover.shape[0]
    groups, my_group = lax.axis_size("dp"), lax.axis_index("dp")
    attended = attend_all(queries, keys, values, segment.reshape(-1, 1, PIECE))
    scale_rows, scale_cols = w_scale.shape
    blocked = w_out.astype(jnp.float32).reshape(scale_rows, HD, scale_cols, w_out.shape[1] // scale_cols)
    weight = (blocked * w_scale[:, None, :, None]).reshape(w_out.shape).astype(jnp.bfloat16)
    partial = lax.dot_general(weight, attended, (((0,), (1,)), ((), ())), preferred_element_type=jnp.float32)
    home = lax.psum_scatter(partial.astype(jnp.bfloat16), "tensor", scatter_dimension=0, tiled=True)
    pieces = home.reshape(home.shape[0], piece_count, PIECE)
    slots = jnp.arange(groups, dtype=jnp.int32)
    goes = (jnp.mod(my_group + handover, groups)[None, :] == slots[:, None]).astype(jnp.bfloat16)
    comes = (jnp.mod(my_group - handover, groups)[:, None] == slots[None, :]).astype(jnp.bfloat16)
    outgoing = jnp.einsum("tj,cjp->tcp", goes, pieces, preferred_element_type=jnp.float32).astype(jnp.bfloat16)
    arrived = lax.all_to_all(outgoing, "dp", split_axis=0, concat_axis=0, tiled=True)
    handed = jnp.einsum("jt,tcp->cjp", comes, arrived, preferred_element_type=jnp.float32).astype(jnp.bfloat16)
    return handed.reshape(home.shape[0], row_count)


ORDERS = ((2, 1, 3), (2, 3, 0), (1, 3, 0), (2, 1, 0))


def local(queries, keys, values, segment, w_out, w_scale, handover):
    fits = (
        lax.axis_size("dp") == 4
        and lax.axis_size("tensor") == 4
        and handover.shape[0] == 3
        and w_out.shape == (1536, 4 * 1280)
        and queries.shape[0] == 3 * PIECE
    )
    if not fits:
        return general(queries, keys, values, segment, w_out, w_scale, handover)
    meta = jnp.concatenate([lax.axis_index("tensor").astype(jnp.int32)[None], handover])
    missing = 6 - jnp.sum(handover)
    branches = [functools.partial(pipeline, order) for order in ORDERS]
    return lax.switch(
        missing, branches, meta, queries, keys, values, segment.reshape(-1, 1, PIECE), w_out, w_scale
    )


def solution(mesh):
    return jax.shard_map(
        local,
        mesh=mesh,
        in_specs=(
            P(("parts", "dp"), "tensor"),
            P(("parts", "dp"), "tensor"),
            P(("parts", "dp"), "tensor"),
            P(("parts", "dp")),
            P("tensor", None),
            P("tensor", None),
            P("parts"),
        ),
        out_specs=P("tensor", ("parts", "dp")),
        check_vma=False,
    )
```

```python
import functools

import jax
import jax.numpy as jnp
from jax import lax
from jax.experimental import pallas as pl
from jax.experimental.pallas import tpu as pltpu
from jax.sharding import PartitionSpec as P

HD = 128
PIECE = 256
WIDE = 256
NEG = -1e30
LOG2E = 1.4426950408889634
VMEM = 16 * 1024 * 1024
HEADS_STEP = 4

ANY = pl.BlockSpec(memory_space=pl.ANY)


def params():
    return pltpu.CompilerParams(vmem_limit_bytes=VMEM)


def attend_heads(heads, q_ref, k_ref, v_ref, bias, o_ref, first=0):
    ones = jnp.ones((PIECE, HD), jnp.bfloat16)
    for h in range(first, first + heads):
        cols = slice(h * HD, (h + 1) * HD)
        scores = lax.dot_general(
            q_ref[:, cols], k_ref[:, cols], (((1,), (1,)), ((), ())), preferred_element_type=jnp.float32
        )
        scores = scores * (LOG2E * HD ** -0.5) + bias
        top = jnp.max(scores, axis=1, keepdims=True)
        weights = jnp.exp2(scores - top).astype(jnp.bfloat16)
        both = jnp.concatenate([v_ref[:, cols], ones], axis=1)
        mixed = jnp.dot(weights, both, preferred_element_type=jnp.float32)
        o_ref[:, cols] = (mixed[:, :HD] / mixed[:, HD:]).astype(jnp.bfloat16)


def segment_bias(numbers):
    across = jnp.broadcast_to(numbers.astype(jnp.float32), (PIECE, PIECE))
    return jnp.where(across == jnp.transpose(across), 0.0, NEG)


def missing(meta_ref):
    return 6 - (meta_ref[1] + meta_ref[2] + meta_ref[3])


def slot_distance(meta_ref, slot):
    gone = missing(meta_ref)
    passed = gone == SHIFTS[0]
    for shift in SHIFTS[1:slot + 1]:
        passed = jnp.logical_or(passed, gone == shift)
    return jnp.where(passed, (SHIFTS + (0,))[slot + 1], SHIFTS[slot])


def piece_at(meta_ref, distance):
    piece = jnp.where(meta_ref[1] == distance, 0, jnp.where(meta_ref[2] == distance, 1, 2))
    return pl.multiple_of(piece * PIECE, PIECE)


def scaled_product(a_ref, w_ref, s_ref, local_col, global_col):
    rows = []
    for kb in range(w_ref.shape[0] // HD):
        blocks = []
        for fb in range(WIDE // HD):
            tile = w_ref[kb * HD:(kb + 1) * HD, local_col + fb * HD:local_col + (fb + 1) * HD]
            scale = s_ref[kb, global_col // HD + fb]
            blocks.append((tile.astype(jnp.float32) * scale).astype(jnp.bfloat16))
        rows.append(jnp.concatenate(blocks, axis=1))
    return jnp.dot(a_ref[...], jnp.concatenate(rows, axis=0), preferred_element_type=jnp.float32)


def spans(me, features, flip, ranges):
    away, home = (me ^ 2) ^ flip, me ^ flip
    return [
        (pl.multiple_of(rank * features + first, HD), width) for first, width in ranges for rank in (away, home)
    ]


def sibling_kernel(features, slot, ranges, cut, attend, meta_ref, *refs):
    refs = list(refs)
    inputs = [refs.pop(0) for _ in range(7 if attend else 4)]
    outs = [refs.pop(0) for _ in range(sum(len(pieces_of(width, cut)) for _, width in ranges))]
    if attend:
        q_hbm, k_hbm, v_hbm, seg_hbm, w_hbm, s_hbm, _ = inputs
        att_hbm = refs.pop(0)
        att, w_ref, s_ref, out, w_sem, o_sem, s_sem, q_ref, k_ref, v_ref, seg_ref, in_sem, seg_sem, att_sem = refs
        first_row = piece_at(meta_ref, slot_distance(meta_ref, slot))
        groups = q_ref.shape[1] // (HEADS_STEP * HD)
        loads = []
        seg_load = pltpu.make_async_copy(seg_hbm.at[pl.ds(first_row // PIECE, 1)], seg_ref, seg_sem)
        seg_load.start()
        for g in range(groups):
            cols = pl.ds(g * HEADS_STEP * HD, HEADS_STEP * HD)
            for i, (source, dest) in enumerate(((q_hbm, q_ref), (k_hbm, k_ref), (v_hbm, v_ref))):
                load = pltpu.make_async_copy(
                    source.at[pl.ds(first_row, PIECE), cols], dest.at[:, cols], in_sem.at[g, i]
                )
                load.start()
                loads.append(load)
    else:
        att_hbm, w_hbm, s_hbm, _ = inputs
        att, w_ref, s_ref, out, w_sem, o_sem, s_sem, att_sem = refs
        att_load = pltpu.make_async_copy(att_hbm, att, att_sem)
        att_load.start()
    scale_load = pltpu.make_async_copy(s_hbm, s_ref, s_sem)
    scale_load.start()
    columns = spans(meta_ref[0], features, 1, ranges)
    w_loads, at = [], 0
    for i, (first, width) in enumerate(columns):
        load = pltpu.make_async_copy(w_hbm.at[:, pl.ds(first, width)], w_ref.at[:, pl.ds(at, width)], w_sem.at[i])
        load.start()
        w_loads.append(load)
        at += width
    if attend:
        seg_load.wait()
        bias = segment_bias(seg_ref[0])
        for g in range(groups):
            for load in loads[3 * g:3 * g + 3]:
                load.wait()
            attend_heads(HEADS_STEP, q_ref, k_ref, v_ref, bias, att, g * HEADS_STEP)
        att_store = pltpu.make_async_copy(att, att_hbm, att_sem)
        att_store.start()
    else:
        att_load.wait()
    scale_load.wait()
    stores, at, done = [], 0, 0
    for i, (first, width) in enumerate(columns):
        w_loads[i].wait()
        for inner in range(0, width, WIDE):
            product = scaled_product(att, w_ref, s_ref, at + inner, first + inner)
            out[:, at + inner:at + inner + WIDE] = product.astype(jnp.bfloat16)
        at += width
        if i % 2:
            for piece in pieces_of(width, cut):
                dest = outs[len(stores)]
                store = pltpu.make_async_copy(out.at[:, pl.ds(done, piece)], dest, o_sem.at[len(stores)])
                store.start()
                stores.append(store)
                done += piece
    for store in stores:
        store.wait()
    if attend:
        att_store.wait()


def pieces_of(width, cut):
    return [2 * width] if cut is None else [cut] * (2 * width // cut)


def sibling_part(meta, slot, ranges, cut, inputs, attended, w_out, w_scale, features, token, cost):
    rows, depth = PIECE, w_out.shape[0]
    widths = [piece for _, width in ranges for piece in pieces_of(width, cut)]
    attend = attended is None
    bf16 = jnp.bfloat16
    scratch = [
        pltpu.VMEM((rows, depth), bf16),
        pltpu.VMEM((depth, sum(widths)), bf16),
        pltpu.SMEM(w_scale.shape, jnp.float32),
        pltpu.VMEM((rows, sum(widths)), bf16),
        pltpu.SemaphoreType.DMA((2 * len(ranges),)),
        pltpu.SemaphoreType.DMA((len(widths),)),
        pltpu.SemaphoreType.DMA,
    ]
    shapes = [jax.ShapeDtypeStruct((rows, width), bf16) for width in widths]
    if attend:
        scratch += [pltpu.VMEM((rows, depth), bf16)] * 3
        scratch += [pltpu.VMEM((1, 1, PIECE), jnp.int32)]
        scratch += [pltpu.SemaphoreType.DMA((depth // (HEADS_STEP * HD), 3)), pltpu.SemaphoreType.DMA]
        shapes.append(jax.ShapeDtypeStruct((rows, depth), bf16))
    operands = (tuple(inputs) if attend else (attended,)) + (w_out, w_scale, token)
    result = pl.pallas_call(
        functools.partial(sibling_kernel, features, slot, ranges, cut, attend),
        grid_spec=pltpu.PrefetchScalarGridSpec(
            num_scalar_prefetch=1,
            grid=(1,),
            in_specs=[ANY] * len(operands),
            out_specs=[ANY] * len(shapes),
            scratch_shapes=scratch + [pltpu.SemaphoreType.DMA],
        ),
        out_shape=shapes,
        compiler_params=params(),
        cost_estimate=cost,
    )(meta, *operands)
    parts, at = [], 0
    for _, width in ranges:
        count = len(pieces_of(width, cut))
        parts.append(result[at:at + count])
        at += count
    return parts, result[-1] if attend else attended


def own_kernel(features, chunk, count, meta_ref, att_hbm, w_hbm, s_hbm, *refs):
    received, refs = refs[:count], refs[count + 1:]
    send_hbm, keep_hbm, att, w_ref, s_ref, r_ref, out, w_sem, r_sem, o_sem, s_sem, att_sem = refs
    width = chunk[1]
    att_load = pltpu.make_async_copy(att_hbm, att, att_sem)
    att_load.start()
    scale_load = pltpu.make_async_copy(s_hbm, s_ref, s_sem)
    scale_load.start()
    columns = spans(meta_ref[0], features, 0, [chunk])
    loads, at = [], 0
    for i, (first, _) in enumerate(columns):
        load = pltpu.make_async_copy(
            w_hbm.at[:, pl.ds(first, width)], w_ref.at[:, pl.ds(i * width, width)], w_sem.at[i]
        )
        load.start()
        loads.append(load)
    received_loads = []
    for i, source in enumerate(received):
        load = pltpu.make_async_copy(source, r_ref.at[:, pl.ds(at, source.shape[1])], r_sem.at[i])
        load.start()
        received_loads.append(load)
        at += source.shape[1]
    att_load.wait()
    scale_load.wait()
    for load in received_loads:
        load.wait()
    stores = []
    for i, (first, _) in enumerate(columns):
        loads[i].wait()
        for inner in range(0, width, WIDE):
            cols = slice(i * width + inner, i * width + inner + WIDE)
            product = scaled_product(att, w_ref, s_ref, i * width + inner, first + inner)
            out[:, cols] = (product + r_ref[:, cols].astype(jnp.float32)).astype(jnp.bfloat16)
        store = pltpu.make_async_copy(out.at[:, pl.ds(i * width, width)], (send_hbm, keep_hbm)[i], o_sem.at[i])
        store.start()
        stores.append(store)
    for store in stores:
        store.wait()


def own_part(meta, chunk, attended, w_out, w_scale, received, features, token, cost):
    rows, depth = attended.shape
    width = chunk[1]
    bf16 = jnp.bfloat16
    return pl.pallas_call(
        functools.partial(own_kernel, features, chunk, len(received)),
        grid_spec=pltpu.PrefetchScalarGridSpec(
            num_scalar_prefetch=1,
            grid=(1,),
            in_specs=[ANY] * (4 + len(received)),
            out_specs=[ANY] * 2,
            scratch_shapes=[
                pltpu.VMEM((rows, depth), bf16),
                pltpu.VMEM((depth, 2 * width), bf16),
                pltpu.SMEM(w_scale.shape, jnp.float32),
                pltpu.VMEM((rows, 2 * width), bf16),
                pltpu.VMEM((rows, 2 * width), bf16),
                pltpu.SemaphoreType.DMA((2,)),
                pltpu.SemaphoreType.DMA((len(received),)),
                pltpu.SemaphoreType.DMA((2,)),
                pltpu.SemaphoreType.DMA,
                pltpu.SemaphoreType.DMA,
            ],
        ),
        out_shape=[jax.ShapeDtypeStruct((rows, width), bf16)] * 2,
        compiler_params=params(),
        cost_estimate=cost,
    )(meta, attended, w_out, w_scale, *received, token)


def finish_kernel(slot, first, into, arrivals, meta_ref, *refs):
    refs = list(refs)
    sem, out = refs.pop(), refs.pop()
    whole = refs.pop() if into else None
    pair = [refs.pop(0), refs.pop(0)] if slot is not None else []
    before = refs.pop(0) if slot else None
    stores = []
    for i, (shift, at) in enumerate(arrivals):
        source = refs.pop(0)
        dest = whole.at[pl.ds(at, source.shape[0]), pl.ds(piece_at(meta_ref, shift), PIECE)]
        stores.append((missing(meta_ref) != shift, pltpu.make_async_copy(source, dest, sem.at[3 + i])))
    for exists, store in stores:
        pl.when(exists)(store.start)
    if slot is not None:
        keep_ref, r_ref = pair
        width = keep_ref.shape[1]
        for at in range(0, width, WIDE):
            cols = slice(at, at + WIDE)
            total = keep_ref[:, cols].astype(jnp.float32) + r_ref[:, cols].astype(jnp.float32)
            out[cols, :] = jnp.transpose(total.astype(jnp.bfloat16))
        last = slot == len(SHIFTS) - 1
        results = refs[-2:] if slot and not last else refs[-1:]
        sent = results[0]
        own = pltpu.make_async_copy(out, sent, sem.at[0])
        if slot == 0:
            own.start()
        else:
            moved = slot_distance(meta_ref, slot) == SHIFTS[slot]
            pl.when(moved)(own.start)
            pl.when(jnp.logical_not(moved))(pltpu.make_async_copy(before, sent, sem.at[0]).start)
        if slot and not last:
            copy = pltpu.make_async_copy(out, results[1], sem.at[1])
            copy.start()
            copy.wait()
        if last:
            dest = whole.at[pl.ds(first, width), pl.ds(piece_at(meta_ref, 0), PIECE)]
            stay = pltpu.make_async_copy(out, dest, sem.at[2])
            pl.when(jnp.logical_not(moved))(stay.start)
            pl.when(jnp.logical_not(moved))(stay.wait)
        own.wait()
    for exists, store in stores:
        pl.when(exists)(store.wait)


def finish(meta, slot, first, pair, before, arrivals, whole, target, token, cost):
    last = slot == len(SHIFTS) - 1
    into = bool(arrivals) or last
    arrays = list(pair) + ([before] if slot else []) + [chunk for _, _, chunk in arrivals]
    specs = [pl.BlockSpec(array.shape, lambda g, meta: (0, 0)) for array in arrays]
    if token is not whole:
        arrays, specs = arrays + [token], specs + [ANY]
    aliases = {}
    scratch_shape = (pair[0].shape[1], PIECE) if pair else (16, HD)
    shapes = []
    if slot is not None:
        shapes = [jax.ShapeDtypeStruct(scratch_shape, jnp.bfloat16)] * (2 if slot and not last else 1)
    if into:
        if whole is not None:
            aliases = {1 + len(arrays): len(shapes)}
            arrays, specs = arrays + [whole], specs + [ANY]
        shapes.append(target)
    result = pl.pallas_call(
        functools.partial(finish_kernel, slot, first, into, [a[:2] for a in arrivals]),
        grid_spec=pltpu.PrefetchScalarGridSpec(
            num_scalar_prefetch=1,
            grid=(1,),
            in_specs=specs,
            out_specs=[ANY] * len(shapes),
            scratch_shapes=[
                pltpu.VMEM(scratch_shape, jnp.bfloat16), pltpu.SemaphoreType.DMA((3 + len(arrivals),))
            ],
        ),
        out_shape=shapes,
        input_output_aliases=aliases,
        compiler_params=params(),
        cost_estimate=cost,
    )(meta, *arrays)
    sent = result[0] if slot is not None else None
    return sent, result[1] if slot and not last else sent, result[-1] if into else whole


SHORT = pl.CostEstimate(flops=1000, bytes_accessed=1000, transcendentals=0)
LONG = pl.CostEstimate(flops=5 * 10**10, bytes_accessed=1000, transcendentals=0)

SHIFTS = (2, 1, 3)
CHUNKS = ((0, 0, 768), (0, 768, 512), (1, 0, 768), (1, 768, 512), (2, 0, 768), (2, 768, 512))
SHARES = ((0, (0, 1)), (1, (2, 3)), (2, (4, 5)))
CUT = None
STEPS = (
    "s0", "o0", "s1", "f0", "o3", "o2", "p0", "o1", "s2", "f1", "o4", "f2", "p1", "f3", "p2", "o5", "f4",
    "p3", "f5", "p4", "p5",
)
COUNT_LONG = ("f0", "f1", "f3", "f4", "f5",)


def pipeline(meta, queries, keys, values, segment, w_out, w_scale):
    groups = lax.axis_size("dp")
    ranks = lax.axis_size("tensor")
    features = w_out.shape[1] // ranks
    other_core = [(i, i ^ 1) for i in range(ranks)]
    other_chip = [(i, i ^ 2) for i in range(ranks)]
    target = jax.ShapeDtypeStruct((features, queries.shape[0]), jnp.bfloat16)
    inputs = (queries, keys, values, segment)
    attended, from_core, kept, from_chip, finished, arrived = {}, {}, {}, {}, {}, {}
    token, whole, waiting = meta, None, []
    finishes = sum(step[0] == "f" for step in STEPS)

    for step in STEPS:
        kind, index = step[0], int(step[1:])
        cost = LONG if step in COUNT_LONG else SHORT
        if kind == "s":
            slot, members = SHARES[index]
            ranges = [CHUNKS[i][1:] for i in members]
            parts, attended[slot] = sibling_part(
                meta, slot, ranges, CUT, inputs, attended.get(slot), w_out, w_scale, features, token, cost
            )
            token = parts[0][0]
            for i, arrays in zip(members, parts):
                from_core[i] = [lax.ppermute(array, "tensor", other_core) for array in arrays]
            continue
        slot, first, width = CHUNKS[index]
        if kind == "o":
            send, kept[index] = own_part(
                meta, (first, width), attended[slot], w_out, w_scale, from_core[index], features, token, cost
            )
            token = kept[index]
            from_chip[index] = lax.ppermute(send, "tensor", other_chip)
            continue
        if kind == "p":
            waiting.append((SHIFTS[slot], first, arrived[index]))
            if finishes:
                continue
            _, _, whole = finish(meta, None, first, (), None, waiting, whole, target, token, cost)
            token, waiting = whole, []
            continue
        finishes -= 1
        pair, before = (kept[index], from_chip[index]), finished.get((slot - 1, first))
        token, finished[slot, first], whole = finish(
            meta, slot, first, pair, before, waiting, whole, target, token, cost
        )
        waiting = []
        arrived[index] = lax.ppermute(token, "dp", [(i, (i + SHIFTS[slot]) % groups) for i in range(groups)])
    return whole


def attention_kernel(heads, q_ref, k_ref, v_ref, seg_ref, o_ref):
    attend_heads(heads, q_ref, k_ref, v_ref, segment_bias(seg_ref[0]), o_ref)


def attend_all(queries, keys, values, segment):
    rows, width = queries.shape
    heads = HEADS_STEP if (width // HD) % HEADS_STEP == 0 else 1
    block = pl.BlockSpec((PIECE, heads * HD), lambda i, g: (i, g))
    return pl.pallas_call(
        functools.partial(attention_kernel, heads),
        grid=(rows // PIECE, width // (heads * HD)),
        in_specs=[block, block, block, pl.BlockSpec((1, 1, PIECE), lambda i, g: (i, 0, 0))],
        out_specs=block,
        out_shape=jax.ShapeDtypeStruct((rows, width), jnp.bfloat16),
        compiler_params=params(),
    )(queries, keys, values, segment)


def general(queries, keys, values, segment, w_out, w_scale, handover):
    row_count, width = queries.shape
    piece_count = handover.shape[0]
    groups, my_group = lax.axis_size("dp"), lax.axis_index("dp")
    attended = attend_all(queries, keys, values, segment.reshape(-1, 1, PIECE))
    scale_rows, scale_cols = w_scale.shape
    blocked = w_out.astype(jnp.float32).reshape(scale_rows, HD, scale_cols, w_out.shape[1] // scale_cols)
    weight = (blocked * w_scale[:, None, :, None]).reshape(w_out.shape).astype(jnp.bfloat16)
    partial = lax.dot_general(weight, attended, (((0,), (1,)), ((), ())), preferred_element_type=jnp.float32)
    home = lax.psum_scatter(partial.astype(jnp.bfloat16), "tensor", scatter_dimension=0, tiled=True)
    pieces = home.reshape(home.shape[0], piece_count, PIECE)
    slots = jnp.arange(groups, dtype=jnp.int32)
    goes = (jnp.mod(my_group + handover, groups)[None, :] == slots[:, None]).astype(jnp.bfloat16)
    comes = (jnp.mod(my_group - handover, groups)[:, None] == slots[None, :]).astype(jnp.bfloat16)
    outgoing = jnp.einsum("tj,cjp->tcp", goes, pieces, preferred_element_type=jnp.float32).astype(jnp.bfloat16)
    arrived = lax.all_to_all(outgoing, "dp", split_axis=0, concat_axis=0, tiled=True)
    handed = jnp.einsum("jt,tcp->cjp", comes, arrived, preferred_element_type=jnp.float32).astype(jnp.bfloat16)
    return handed.reshape(home.shape[0], row_count)


def local(queries, keys, values, segment, w_out, w_scale, handover):
    fits = (
        lax.axis_size("dp") == 4
        and lax.axis_size("tensor") == 4
        and handover.shape[0] == 3
        and w_out.shape == (1536, 4 * 1280)
        and queries.shape[0] == 3 * PIECE
    )
    if not fits:
        return general(queries, keys, values, segment, w_out, w_scale, handover)
    meta = jnp.concatenate([lax.axis_index("tensor").astype(jnp.int32)[None], handover])
    return pipeline(meta, queries, keys, values, segment.reshape(-1, 1, PIECE), w_out, w_scale)


def solution(mesh):
    return jax.shard_map(
        local,
        mesh=mesh,
        in_specs=(
            P(("parts", "dp"), "tensor"),
            P(("parts", "dp"), "tensor"),
            P(("parts", "dp"), "tensor"),
            P(("parts", "dp")),
            P("tensor", None),
            P("tensor", None),
            P("parts"),
        ),
        out_specs=P("tensor", ("parts", "dp")),
        check_vma=False,
    )
```

```python
import functools

import jax
import jax.numpy as jnp
from jax import lax
from jax.experimental import pallas as pl
from jax.experimental.pallas import tpu as pltpu
from jax.sharding import PartitionSpec as P

HD = 128
PIECE = 256
WIDE = 256
NEG = -1e30
LOG2E = 1.4426950408889634
VMEM = 50 * 1024 * 1024
HEADS_STEP = 4

ANY = pl.BlockSpec(memory_space=pl.ANY)


def params():
    return pltpu.CompilerParams(vmem_limit_bytes=VMEM)


def attend_heads(heads, q_ref, k_ref, v_ref, bias, o_ref, first=0):
    ones = jnp.ones((PIECE, HD), jnp.bfloat16)
    for h in range(first, first + heads):
        cols = slice(h * HD, (h + 1) * HD)
        scores = lax.dot_general(
            q_ref[:, cols], k_ref[:, cols], (((1,), (1,)), ((), ())), preferred_element_type=jnp.float32
        )
        scores = scores * (LOG2E * HD ** -0.5) + bias
        top = jnp.max(scores, axis=1, keepdims=True)
        weights = jnp.exp2(scores - top).astype(jnp.bfloat16)
        both = jnp.concatenate([v_ref[:, cols], ones], axis=1)
        mixed = jnp.dot(weights, both, preferred_element_type=jnp.float32)
        o_ref[:, cols] = (mixed[:, :HD] / mixed[:, HD:]).astype(jnp.bfloat16)


def segment_bias(numbers):
    across = jnp.broadcast_to(numbers.astype(jnp.float32), (PIECE, PIECE))
    return jnp.where(across == jnp.transpose(across), 0.0, NEG)


def missing(meta_ref):
    return 6 - (meta_ref[1] + meta_ref[2] + meta_ref[3])


def slot_distance(meta_ref, slot):
    gone = missing(meta_ref)
    passed = gone == SHIFTS[0]
    for shift in SHIFTS[1:slot + 1]:
        passed = jnp.logical_or(passed, gone == shift)
    return jnp.where(passed, (SHIFTS + (0,))[slot + 1], SHIFTS[slot])


def piece_at(meta_ref, distance):
    piece = jnp.where(meta_ref[1] == distance, 0, jnp.where(meta_ref[2] == distance, 1, 2))
    return pl.multiple_of(piece * PIECE, PIECE)


def scaled_product(a_ref, w_ref, s_ref, local_col, global_col):
    rows = []
    for kb in range(w_ref.shape[0] // HD):
        blocks = []
        for fb in range(WIDE // HD):
            tile = w_ref[kb * HD:(kb + 1) * HD, local_col + fb * HD:local_col + (fb + 1) * HD]
            scale = s_ref[kb, global_col // HD + fb]
            blocks.append((tile.astype(jnp.float32) * scale).astype(jnp.bfloat16))
        rows.append(jnp.concatenate(blocks, axis=1))
    return jnp.dot(a_ref[...], jnp.concatenate(rows, axis=0), preferred_element_type=jnp.float32)


def spans(me, features, flip, ranges):
    away, home = (me ^ 2) ^ flip, me ^ flip
    return [
        (pl.multiple_of(rank * features + first, HD), width) for first, width in ranges for rank in (away, home)
    ]


def sibling_kernel(features, slot, ranges, cut, attend, meta_ref, *refs):
    refs = list(refs)
    inputs = [refs.pop(0) for _ in range(7 if attend else 4)]
    outs = [refs.pop(0) for _ in range(sum(len(pieces_of(width, cut)) for _, width in ranges))]
    if attend:
        q_hbm, k_hbm, v_hbm, seg_hbm, w_hbm, s_hbm, _ = inputs
        att_hbm = refs.pop(0)
        att, w_ref, s_ref, out, w_sem, o_sem, s_sem, q_ref, k_ref, v_ref, seg_ref, in_sem, seg_sem, att_sem = refs
        first_row = piece_at(meta_ref, slot_distance(meta_ref, slot))
        groups = q_ref.shape[1] // (HEADS_STEP * HD)
        loads = []
        seg_load = pltpu.make_async_copy(seg_hbm.at[pl.ds(first_row // PIECE, 1)], seg_ref, seg_sem)
        seg_load.start()
        for g in range(groups):
            cols = pl.ds(g * HEADS_STEP * HD, HEADS_STEP * HD)
            for i, (source, dest) in enumerate(((q_hbm, q_ref), (k_hbm, k_ref), (v_hbm, v_ref))):
                load = pltpu.make_async_copy(
                    source.at[pl.ds(first_row, PIECE), cols], dest.at[:, cols], in_sem.at[g, i]
                )
                load.start()
                loads.append(load)
    else:
        att_hbm, w_hbm, s_hbm, _ = inputs
        att, w_ref, s_ref, out, w_sem, o_sem, s_sem, att_sem = refs
        att_load = pltpu.make_async_copy(att_hbm, att, att_sem)
        att_load.start()
    scale_load = pltpu.make_async_copy(s_hbm, s_ref, s_sem)
    scale_load.start()
    columns = spans(meta_ref[0], features, 1, ranges)
    w_loads, at = [], 0
    for i, (first, width) in enumerate(columns):
        load = pltpu.make_async_copy(w_hbm.at[:, pl.ds(first, width)], w_ref.at[:, pl.ds(at, width)], w_sem.at[i])
        load.start()
        w_loads.append(load)
        at += width
    if attend:
        seg_load.wait()
        bias = segment_bias(seg_ref[0])
        for g in range(groups):
            for load in loads[3 * g:3 * g + 3]:
                load.wait()
            attend_heads(HEADS_STEP, q_ref, k_ref, v_ref, bias, att, g * HEADS_STEP)
        att_store = pltpu.make_async_copy(att, att_hbm, att_sem)
        att_store.start()
    else:
        att_load.wait()
    scale_load.wait()
    stores, at, done = [], 0, 0
    for i, (first, width) in enumerate(columns):
        w_loads[i].wait()
        for inner in range(0, width, WIDE):
            product = scaled_product(att, w_ref, s_ref, at + inner, first + inner)
            out[:, at + inner:at + inner + WIDE] = product.astype(jnp.bfloat16)
        at += width
        if i % 2:
            for piece in pieces_of(width, cut):
                dest = outs[len(stores)]
                store = pltpu.make_async_copy(out.at[:, pl.ds(done, piece)], dest, o_sem.at[len(stores)])
                store.start()
                stores.append(store)
                done += piece
    for store in stores:
        store.wait()
    if attend:
        att_store.wait()


def pieces_of(width, cut):
    return [2 * width] if cut is None else [cut] * (2 * width // cut)


def sibling_part(meta, slot, ranges, cut, inputs, attended, w_out, w_scale, features, token, cost):
    rows, depth = PIECE, w_out.shape[0]
    widths = [piece for _, width in ranges for piece in pieces_of(width, cut)]
    attend = attended is None
    bf16 = jnp.bfloat16
    scratch = [
        pltpu.VMEM((rows, depth), bf16),
        pltpu.VMEM((depth, sum(widths)), bf16),
        pltpu.SMEM(w_scale.shape, jnp.float32),
        pltpu.VMEM((rows, sum(widths)), bf16),
        pltpu.SemaphoreType.DMA((2 * len(ranges),)),
        pltpu.SemaphoreType.DMA((len(widths),)),
        pltpu.SemaphoreType.DMA,
    ]
    shapes = [jax.ShapeDtypeStruct((rows, width), bf16) for width in widths]
    if attend:
        scratch += [pltpu.VMEM((rows, depth), bf16)] * 3
        scratch += [pltpu.VMEM((1, 1, PIECE), jnp.int32)]
        scratch += [pltpu.SemaphoreType.DMA((depth // (HEADS_STEP * HD), 3)), pltpu.SemaphoreType.DMA]
        shapes.append(jax.ShapeDtypeStruct((rows, depth), bf16))
    operands = (tuple(inputs) if attend else (attended,)) + (w_out, w_scale, token)
    result = pl.pallas_call(
        functools.partial(sibling_kernel, features, slot, ranges, cut, attend),
        grid_spec=pltpu.PrefetchScalarGridSpec(
            num_scalar_prefetch=1,
            grid=(1,),
            in_specs=[ANY] * len(operands),
            out_specs=[ANY] * len(shapes),
            scratch_shapes=scratch + [pltpu.SemaphoreType.DMA],
        ),
        out_shape=shapes,
        compiler_params=params(),
        cost_estimate=cost,
    )(meta, *operands)
    parts, at = [], 0
    for _, width in ranges:
        count = len(pieces_of(width, cut))
        parts.append(result[at:at + count])
        at += count
    return parts, result[-1] if attend else attended


def own_kernel(features, chunk, count, meta_ref, att_hbm, w_hbm, s_hbm, *refs):
    received, refs = refs[:count], refs[count + 1:]
    send_hbm, keep_hbm, att, w_ref, s_ref, r_ref, out, w_sem, r_sem, o_sem, s_sem, att_sem = refs
    width = chunk[1]
    att_load = pltpu.make_async_copy(att_hbm, att, att_sem)
    att_load.start()
    scale_load = pltpu.make_async_copy(s_hbm, s_ref, s_sem)
    scale_load.start()
    columns = spans(meta_ref[0], features, 0, [chunk])
    loads, at = [], 0
    for i, (first, _) in enumerate(columns):
        load = pltpu.make_async_copy(
            w_hbm.at[:, pl.ds(first, width)], w_ref.at[:, pl.ds(i * width, width)], w_sem.at[i]
        )
        load.start()
        loads.append(load)
    received_loads = []
    for i, source in enumerate(received):
        load = pltpu.make_async_copy(source, r_ref.at[:, pl.ds(at, source.shape[1])], r_sem.at[i])
        load.start()
        received_loads.append(load)
        at += source.shape[1]
    att_load.wait()
    scale_load.wait()
    for load in received_loads:
        load.wait()
    stores = []
    for i, (first, _) in enumerate(columns):
        loads[i].wait()
        for inner in range(0, width, WIDE):
            cols = slice(i * width + inner, i * width + inner + WIDE)
            product = scaled_product(att, w_ref, s_ref, i * width + inner, first + inner)
            out[:, cols] = (product + r_ref[:, cols].astype(jnp.float32)).astype(jnp.bfloat16)
        store = pltpu.make_async_copy(out.at[:, pl.ds(i * width, width)], (send_hbm, keep_hbm)[i], o_sem.at[i])
        store.start()
        stores.append(store)
    for store in stores:
        store.wait()


def own_part(meta, chunk, attended, w_out, w_scale, received, features, token, cost):
    rows, depth = attended.shape
    width = chunk[1]
    bf16 = jnp.bfloat16
    return pl.pallas_call(
        functools.partial(own_kernel, features, chunk, len(received)),
        grid_spec=pltpu.PrefetchScalarGridSpec(
            num_scalar_prefetch=1,
            grid=(1,),
            in_specs=[ANY] * (4 + len(received)),
            out_specs=[ANY] * 2,
            scratch_shapes=[
                pltpu.VMEM((rows, depth), bf16),
                pltpu.VMEM((depth, 2 * width), bf16),
                pltpu.SMEM(w_scale.shape, jnp.float32),
                pltpu.VMEM((rows, 2 * width), bf16),
                pltpu.VMEM((rows, 2 * width), bf16),
                pltpu.SemaphoreType.DMA((2,)),
                pltpu.SemaphoreType.DMA((len(received),)),
                pltpu.SemaphoreType.DMA((2,)),
                pltpu.SemaphoreType.DMA,
                pltpu.SemaphoreType.DMA,
            ],
        ),
        out_shape=[jax.ShapeDtypeStruct((rows, width), bf16)] * 2,
        compiler_params=params(),
        cost_estimate=cost,
    )(meta, attended, w_out, w_scale, *received, token)


def finish_kernel(slot, first, into, arrivals, meta_ref, *refs):
    refs = list(refs)
    sem, out = refs.pop(), refs.pop()
    whole = refs.pop() if into else None
    pair = [refs.pop(0), refs.pop(0)] if slot is not None else []
    before = refs.pop(0) if slot else None
    stores = []
    for i, (shift, at) in enumerate(arrivals):
        source = refs.pop(0)
        dest = whole.at[pl.ds(at, source.shape[0]), pl.ds(piece_at(meta_ref, shift), PIECE)]
        stores.append((missing(meta_ref) != shift, pltpu.make_async_copy(source, dest, sem.at[3 + i])))
    for exists, store in stores:
        pl.when(exists)(store.start)
    if slot is not None:
        keep_ref, r_ref = pair
        width = keep_ref.shape[1]
        for at in range(0, width, WIDE):
            cols = slice(at, at + WIDE)
            total = keep_ref[:, cols].astype(jnp.float32) + r_ref[:, cols].astype(jnp.float32)
            out[cols, :] = jnp.transpose(total.astype(jnp.bfloat16))
        last = slot == len(SHIFTS) - 1
        results = refs[-2:] if slot and not last else refs[-1:]
        sent = results[0]
        own = pltpu.make_async_copy(out, sent, sem.at[0])
        if slot == 0:
            own.start()
        else:
            moved = slot_distance(meta_ref, slot) == SHIFTS[slot]
            pl.when(moved)(own.start)
            pl.when(jnp.logical_not(moved))(pltpu.make_async_copy(before, sent, sem.at[0]).start)
        if slot and not last:
            copy = pltpu.make_async_copy(out, results[1], sem.at[1])
            copy.start()
            copy.wait()
        if last:
            dest = whole.at[pl.ds(first, width), pl.ds(piece_at(meta_ref, 0), PIECE)]
            stay = pltpu.make_async_copy(out, dest, sem.at[2])
            pl.when(jnp.logical_not(moved))(stay.start)
            pl.when(jnp.logical_not(moved))(stay.wait)
        own.wait()
    for exists, store in stores:
        pl.when(exists)(store.wait)


def finish(meta, slot, first, pair, before, arrivals, whole, target, token, cost):
    last = slot == len(SHIFTS) - 1
    into = bool(arrivals) or last
    arrays = list(pair) + ([before] if slot else []) + [chunk for _, _, chunk in arrivals]
    specs = [pl.BlockSpec(array.shape, lambda g, meta: (0, 0)) for array in arrays]
    if token is not whole:
        arrays, specs = arrays + [token], specs + [ANY]
    aliases = {}
    scratch_shape = (pair[0].shape[1], PIECE) if pair else (16, HD)
    shapes = []
    if slot is not None:
        shapes = [jax.ShapeDtypeStruct(scratch_shape, jnp.bfloat16)] * (2 if slot and not last else 1)
    if into:
        if whole is not None:
            aliases = {1 + len(arrays): len(shapes)}
            arrays, specs = arrays + [whole], specs + [ANY]
        shapes.append(target)
    result = pl.pallas_call(
        functools.partial(finish_kernel, slot, first, into, [a[:2] for a in arrivals]),
        grid_spec=pltpu.PrefetchScalarGridSpec(
            num_scalar_prefetch=1,
            grid=(1,),
            in_specs=specs,
            out_specs=[ANY] * len(shapes),
            scratch_shapes=[
                pltpu.VMEM(scratch_shape, jnp.bfloat16), pltpu.SemaphoreType.DMA((3 + len(arrivals),))
            ],
        ),
        out_shape=shapes,
        input_output_aliases=aliases,
        compiler_params=params(),
        cost_estimate=cost,
    )(meta, *arrays)
    sent = result[0] if slot is not None else None
    return sent, result[1] if slot and not last else sent, result[-1] if into else whole


SHORT = pl.CostEstimate(flops=1000, bytes_accessed=1000, transcendentals=0)
LONG = pl.CostEstimate(flops=5 * 10**10, bytes_accessed=1000, transcendentals=0)

SHIFTS = (2, 3, 1)
CHUNKS = ((0, 0, 768), (0, 768, 512), (1, 0, 768), (1, 768, 512), (2, 0, 768), (2, 768, 512))
SHARES = ((0, (0, 1)), (1, (2, 3)), (2, (4, 5)))
CUT = None
STEPS = (
    "s0", "o1", "o0", "f1", "s1", "p1", "s2", "f0", "o4", "p0", "o3", "o2", "f3", "o5", "f2", "p3", "f4",
    "p2", "f5", "p4", "p5",
)
COUNT_LONG = ("f0", "f1", "f3", "f4", "o0", "o1", "o4", "s0",)


def pipeline(meta, queries, keys, values, segment, w_out, w_scale):
    groups = lax.axis_size("dp")
    ranks = lax.axis_size("tensor")
    features = w_out.shape[1] // ranks
    other_core = [(i, i ^ 1) for i in range(ranks)]
    other_chip = [(i, i ^ 2) for i in range(ranks)]
    target = jax.ShapeDtypeStruct((features, queries.shape[0]), jnp.bfloat16)
    inputs = (queries, keys, values, segment)
    attended, from_core, kept, from_chip, finished, arrived = {}, {}, {}, {}, {}, {}
    token, whole, waiting = meta, None, []
    finishes = sum(step[0] == "f" for step in STEPS)

    for step in STEPS:
        kind, index = step[0], int(step[1:])
        cost = LONG if step in COUNT_LONG else SHORT
        if kind == "s":
            slot, members = SHARES[index]
            ranges = [CHUNKS[i][1:] for i in members]
            parts, attended[slot] = sibling_part(
                meta, slot, ranges, CUT, inputs, attended.get(slot), w_out, w_scale, features, token, cost
            )
            token = parts[0][0]
            for i, arrays in zip(members, parts):
                from_core[i] = [lax.ppermute(array, "tensor", other_core) for array in arrays]
            continue
        slot, first, width = CHUNKS[index]
        if kind == "o":
            send, kept[index] = own_part(
                meta, (first, width), attended[slot], w_out, w_scale, from_core[index], features, token, cost
            )
            token = kept[index]
            from_chip[index] = lax.ppermute(send, "tensor", other_chip)
            continue
        if kind == "p":
            waiting.append((SHIFTS[slot], first, arrived[index]))
            if finishes:
                continue
            _, _, whole = finish(meta, None, first, (), None, waiting, whole, target, token, cost)
            token, waiting = whole, []
            continue
        finishes -= 1
        pair, before = (kept[index], from_chip[index]), finished.get((slot - 1, first))
        token, finished[slot, first], whole = finish(
            meta, slot, first, pair, before, waiting, whole, target, token, cost
        )
        waiting = []
        arrived[index] = lax.ppermute(token, "dp", [(i, (i + SHIFTS[slot]) % groups) for i in range(groups)])
    return whole


def attention_kernel(heads, q_ref, k_ref, v_ref, seg_ref, o_ref):
    attend_heads(heads, q_ref, k_ref, v_ref, segment_bias(seg_ref[0]), o_ref)


def attend_all(queries, keys, values, segment):
    rows, width = queries.shape
    heads = HEADS_STEP if (width // HD) % HEADS_STEP == 0 else 1
    block = pl.BlockSpec((PIECE, heads * HD), lambda i, g: (i, g))
    return pl.pallas_call(
        functools.partial(attention_kernel, heads),
        grid=(rows // PIECE, width // (heads * HD)),
        in_specs=[block, block, block, pl.BlockSpec((1, 1, PIECE), lambda i, g: (i, 0, 0))],
        out_specs=block,
        out_shape=jax.ShapeDtypeStruct((rows, width), jnp.bfloat16),
        compiler_params=params(),
    )(queries, keys, values, segment)


def general(queries, keys, values, segment, w_out, w_scale, handover):
    row_count, width = queries.shape
    piece_count = handover.shape[0]
    groups, my_group = lax.axis_size("dp"), lax.axis_index("dp")
    attended = attend_all(queries, keys, values, segment.reshape(-1, 1, PIECE))
    scale_rows, scale_cols = w_scale.shape
    blocked = w_out.astype(jnp.float32).reshape(scale_rows, HD, scale_cols, w_out.shape[1] // scale_cols)
    weight = (blocked * w_scale[:, None, :, None]).reshape(w_out.shape).astype(jnp.bfloat16)
    partial = lax.dot_general(weight, attended, (((0,), (1,)), ((), ())), preferred_element_type=jnp.float32)
    home = lax.psum_scatter(partial.astype(jnp.bfloat16), "tensor", scatter_dimension=0, tiled=True)
    pieces = home.reshape(home.shape[0], piece_count, PIECE)
    slots = jnp.arange(groups, dtype=jnp.int32)
    goes = (jnp.mod(my_group + handover, groups)[None, :] == slots[:, None]).astype(jnp.bfloat16)
    comes = (jnp.mod(my_group - handover, groups)[:, None] == slots[None, :]).astype(jnp.bfloat16)
    outgoing = jnp.einsum("tj,cjp->tcp", goes, pieces, preferred_element_type=jnp.float32).astype(jnp.bfloat16)
    arrived = lax.all_to_all(outgoing, "dp", split_axis=0, concat_axis=0, tiled=True)
    handed = jnp.einsum("jt,tcp->cjp", comes, arrived, preferred_element_type=jnp.float32).astype(jnp.bfloat16)
    return handed.reshape(home.shape[0], row_count)


def local(queries, keys, values, segment, w_out, w_scale, handover):
    fits = (
        lax.axis_size("dp") == 4
        and lax.axis_size("tensor") == 4
        and handover.shape[0] == 3
        and w_out.shape == (1536, 4 * 1280)
        and queries.shape[0] == 3 * PIECE
    )
    if not fits:
        return general(queries, keys, values, segment, w_out, w_scale, handover)
    meta = jnp.concatenate([lax.axis_index("tensor").astype(jnp.int32)[None], handover])
    return pipeline(meta, queries, keys, values, segment.reshape(-1, 1, PIECE), w_out, w_scale)


def solution(mesh):
    return jax.shard_map(
        local,
        mesh=mesh,
        in_specs=(
            P(("parts", "dp"), "tensor"),
            P(("parts", "dp"), "tensor"),
            P(("parts", "dp"), "tensor"),
            P(("parts", "dp")),
            P("tensor", None),
            P("tensor", None),
            P("parts"),
        ),
        out_specs=P("tensor", ("parts", "dp")),
        check_vma=False,
    )
```

```python
import functools

import jax
import jax.numpy as jnp
from jax import lax
from jax.experimental import pallas as pl
from jax.experimental.pallas import tpu as pltpu
from jax.sharding import PartitionSpec as P

HD = 128
PIECE = 256
WIDE = 256
NEG = -1e30
LOG2E = 1.4426950408889634
VMEM = 50 * 1024 * 1024
HEADS_STEP = 4

ANY = pl.BlockSpec(memory_space=pl.ANY)
HBM = pl.BlockSpec(memory_space=pltpu.HBM)


def params():
    return pltpu.CompilerParams(vmem_limit_bytes=VMEM)


def attend_heads(heads, q_ref, k_ref, v_ref, bias, o_ref, first=0):
    ones = jnp.ones((PIECE, HD), jnp.bfloat16)
    for h in range(first, first + heads):
        cols = slice(h * HD, (h + 1) * HD)
        scores = lax.dot_general(
            q_ref[:, cols], k_ref[:, cols], (((1,), (1,)), ((), ())), preferred_element_type=jnp.float32
        )
        scores = scores * (LOG2E * HD ** -0.5) + bias
        top = jnp.max(scores, axis=1, keepdims=True)
        weights = jnp.exp2(scores - top).astype(jnp.bfloat16)
        both = jnp.concatenate([v_ref[:, cols], ones], axis=1)
        mixed = jnp.dot(weights, both, preferred_element_type=jnp.float32)
        o_ref[:, cols] = (mixed[:, :HD] / mixed[:, HD:]).astype(jnp.bfloat16)


def segment_bias(numbers):
    across = jnp.broadcast_to(numbers.astype(jnp.float32), (PIECE, PIECE))
    return jnp.where(across == jnp.transpose(across), 0.0, NEG)


def missing(meta_ref):
    return 6 - (meta_ref[1] + meta_ref[2] + meta_ref[3])


def slot_distance(meta_ref, slot):
    gone = missing(meta_ref)
    passed = gone == SHIFTS[0]
    for shift in SHIFTS[1:slot + 1]:
        passed = jnp.logical_or(passed, gone == shift)
    return jnp.where(passed, (SHIFTS + (0,))[slot + 1], SHIFTS[slot])


def piece_at(meta_ref, distance):
    piece = jnp.where(meta_ref[1] == distance, 0, jnp.where(meta_ref[2] == distance, 1, 2))
    return pl.multiple_of(piece * PIECE, PIECE)


def scaled_product(a_ref, w_ref, s_ref, local_col, global_col):
    rows = []
    for kb in range(w_ref.shape[0] // HD):
        blocks = []
        for fb in range(WIDE // HD):
            tile = w_ref[kb * HD:(kb + 1) * HD, local_col + fb * HD:local_col + (fb + 1) * HD]
            scale = s_ref[kb, global_col // HD + fb]
            blocks.append((tile.astype(jnp.float32) * scale).astype(jnp.bfloat16))
        rows.append(jnp.concatenate(blocks, axis=1))
    return jnp.dot(a_ref[...], jnp.concatenate(rows, axis=0), preferred_element_type=jnp.float32)


def spans(me, features, flip, ranges):
    away, home = (me ^ 2) ^ flip, me ^ flip
    return [
        (pl.multiple_of(rank * features + first, HD), width) for first, width in ranges for rank in (away, home)
    ]


def sibling_kernel(features, slot, ranges, cut, attend, meta_ref, *refs):
    refs = list(refs)
    inputs = [refs.pop(0) for _ in range(7 if attend else 4)]
    outs = [refs.pop(0) for _ in range(sum(len(pieces_of(width, cut)) for _, width in ranges))]
    if attend:
        q_hbm, k_hbm, v_hbm, seg_hbm, w_hbm, s_hbm, _ = inputs
        att_hbm = refs.pop(0)
        att, w_ref, s_ref, out, w_sem, o_sem, s_sem, q_ref, k_ref, v_ref, seg_ref, in_sem, seg_sem, att_sem = refs
        first_row = piece_at(meta_ref, slot_distance(meta_ref, slot))
        groups = q_ref.shape[1] // (HEADS_STEP * HD)
        loads = []
        seg_load = pltpu.make_async_copy(seg_hbm.at[pl.ds(first_row // PIECE, 1)], seg_ref, seg_sem)
        seg_load.start()
        for g in range(groups):
            cols = pl.ds(g * HEADS_STEP * HD, HEADS_STEP * HD)
            for i, (source, dest) in enumerate(((q_hbm, q_ref), (k_hbm, k_ref), (v_hbm, v_ref))):
                load = pltpu.make_async_copy(
                    source.at[pl.ds(first_row, PIECE), cols], dest.at[:, cols], in_sem.at[g, i]
                )
                load.start()
                loads.append(load)
    else:
        att_hbm, w_hbm, s_hbm, _ = inputs
        att, w_ref, s_ref, out, w_sem, o_sem, s_sem, att_sem = refs
        att_load = pltpu.make_async_copy(att_hbm, att, att_sem)
        att_load.start()
    scale_load = pltpu.make_async_copy(s_hbm, s_ref, s_sem)
    scale_load.start()
    columns = spans(meta_ref[0], features, 1, ranges)
    w_loads, at = [], 0
    for i, (first, width) in enumerate(columns):
        load = pltpu.make_async_copy(w_hbm.at[:, pl.ds(first, width)], w_ref.at[:, pl.ds(at, width)], w_sem.at[i])
        load.start()
        w_loads.append(load)
        at += width
    if attend:
        seg_load.wait()
        bias = segment_bias(seg_ref[0])
        for g in range(groups):
            for load in loads[3 * g:3 * g + 3]:
                load.wait()
            attend_heads(HEADS_STEP, q_ref, k_ref, v_ref, bias, att, g * HEADS_STEP)
        att_store = pltpu.make_async_copy(att, att_hbm, att_sem)
        att_store.start()
    else:
        att_load.wait()
    scale_load.wait()
    stores, at, done = [], 0, 0
    for i, (first, width) in enumerate(columns):
        w_loads[i].wait()
        for inner in range(0, width, WIDE):
            product = scaled_product(att, w_ref, s_ref, at + inner, first + inner)
            out[:, at + inner:at + inner + WIDE] = product.astype(jnp.bfloat16)
        at += width
        if i % 2:
            for piece in pieces_of(width, cut):
                dest = outs[len(stores)]
                store = pltpu.make_async_copy(out.at[:, pl.ds(done, piece)], dest, o_sem.at[len(stores)])
                store.start()
                stores.append(store)
                done += piece
    for store in stores:
        store.wait()
    if attend:
        att_store.wait()


def pieces_of(width, cut):
    return [2 * width] if cut is None else [cut] * (2 * width // cut)


def sibling_part(meta, slot, ranges, cut, inputs, attended, w_out, w_scale, features, token, cost):
    rows, depth = PIECE, w_out.shape[0]
    widths = [piece for _, width in ranges for piece in pieces_of(width, cut)]
    attend = attended is None
    bf16 = jnp.bfloat16
    scratch = [
        pltpu.VMEM((rows, depth), bf16),
        pltpu.VMEM((depth, sum(widths)), bf16),
        pltpu.SMEM(w_scale.shape, jnp.float32),
        pltpu.VMEM((rows, sum(widths)), bf16),
        pltpu.SemaphoreType.DMA((2 * len(ranges),)),
        pltpu.SemaphoreType.DMA((len(widths),)),
        pltpu.SemaphoreType.DMA,
    ]
    shapes = [jax.ShapeDtypeStruct((rows, width), bf16) for width in widths]
    if attend:
        scratch += [pltpu.VMEM((rows, depth), bf16)] * 3
        scratch += [pltpu.VMEM((1, 1, PIECE), jnp.int32)]
        scratch += [pltpu.SemaphoreType.DMA((depth // (HEADS_STEP * HD), 3)), pltpu.SemaphoreType.DMA]
        shapes.append(jax.ShapeDtypeStruct((rows, depth), bf16))
    operands = (tuple(inputs) if attend else (attended,)) + (w_out, w_scale, token)
    result = pl.pallas_call(
        functools.partial(sibling_kernel, features, slot, ranges, cut, attend),
        grid_spec=pltpu.PrefetchScalarGridSpec(
            num_scalar_prefetch=1,
            grid=(1,),
            in_specs=([HBM] * 4 if attend else [ANY]) + [HBM, HBM, ANY],
            out_specs=[ANY] * len(shapes),
            scratch_shapes=scratch + [pltpu.SemaphoreType.DMA],
        ),
        out_shape=shapes,
        compiler_params=params(),
        cost_estimate=cost,
    )(meta, *operands)
    parts, at = [], 0
    for _, width in ranges:
        count = len(pieces_of(width, cut))
        parts.append(result[at:at + count])
        at += count
    return parts, result[-1] if attend else attended


def own_kernel(features, chunk, count, meta_ref, att_hbm, w_hbm, s_hbm, *refs):
    received, refs = refs[:count], refs[count + 1:]
    send_hbm, keep_hbm, att, w_ref, s_ref, r_ref, out, w_sem, r_sem, o_sem, s_sem, att_sem = refs
    width = chunk[1]
    att_load = pltpu.make_async_copy(att_hbm, att, att_sem)
    att_load.start()
    scale_load = pltpu.make_async_copy(s_hbm, s_ref, s_sem)
    scale_load.start()
    columns = spans(meta_ref[0], features, 0, [chunk])
    loads, at = [], 0
    for i, (first, _) in enumerate(columns):
        load = pltpu.make_async_copy(
            w_hbm.at[:, pl.ds(first, width)], w_ref.at[:, pl.ds(i * width, width)], w_sem.at[i]
        )
        load.start()
        loads.append(load)
    received_loads = []
    for i, source in enumerate(received):
        load = pltpu.make_async_copy(source, r_ref.at[:, pl.ds(at, source.shape[1])], r_sem.at[i])
        load.start()
        received_loads.append(load)
        at += source.shape[1]
    att_load.wait()
    scale_load.wait()
    for load in received_loads:
        load.wait()
    stores = []
    for i, (first, _) in enumerate(columns):
        loads[i].wait()
        for inner in range(0, width, WIDE):
            cols = slice(i * width + inner, i * width + inner + WIDE)
            product = scaled_product(att, w_ref, s_ref, i * width + inner, first + inner)
            out[:, cols] = (product + r_ref[:, cols].astype(jnp.float32)).astype(jnp.bfloat16)
        store = pltpu.make_async_copy(out.at[:, pl.ds(i * width, width)], (send_hbm, keep_hbm)[i], o_sem.at[i])
        store.start()
        stores.append(store)
    for store in stores:
        store.wait()


def own_part(meta, chunk, attended, w_out, w_scale, received, features, token, cost):
    rows, depth = attended.shape
    width = chunk[1]
    bf16 = jnp.bfloat16
    return pl.pallas_call(
        functools.partial(own_kernel, features, chunk, len(received)),
        grid_spec=pltpu.PrefetchScalarGridSpec(
            num_scalar_prefetch=1,
            grid=(1,),
            in_specs=[ANY, HBM, HBM] + [ANY] * (1 + len(received)),
            out_specs=[ANY] * 2,
            scratch_shapes=[
                pltpu.VMEM((rows, depth), bf16),
                pltpu.VMEM((depth, 2 * width), bf16),
                pltpu.SMEM(w_scale.shape, jnp.float32),
                pltpu.VMEM((rows, 2 * width), bf16),
                pltpu.VMEM((rows, 2 * width), bf16),
                pltpu.SemaphoreType.DMA((2,)),
                pltpu.SemaphoreType.DMA((len(received),)),
                pltpu.SemaphoreType.DMA((2,)),
                pltpu.SemaphoreType.DMA,
                pltpu.SemaphoreType.DMA,
            ],
        ),
        out_shape=[jax.ShapeDtypeStruct((rows, width), bf16)] * 2,
        compiler_params=params(),
        cost_estimate=cost,
    )(meta, attended, w_out, w_scale, *received, token)


def finish_kernel(slot, first, into, arrivals, meta_ref, *refs):
    refs = list(refs)
    sem, out = refs.pop(), refs.pop()
    whole = refs.pop() if into else None
    pair = [refs.pop(0), refs.pop(0)] if slot is not None else []
    before = refs.pop(0) if slot else None
    stores = []
    for i, (shift, at) in enumerate(arrivals):
        source = refs.pop(0)
        dest = whole.at[pl.ds(at, source.shape[0]), pl.ds(piece_at(meta_ref, shift), PIECE)]
        stores.append((missing(meta_ref) != shift, pltpu.make_async_copy(source, dest, sem.at[3 + i])))
    for exists, store in stores:
        pl.when(exists)(store.start)
    if slot is not None:
        keep_ref, r_ref = pair
        width = keep_ref.shape[1]
        for at in range(0, width, WIDE):
            cols = slice(at, at + WIDE)
            total = keep_ref[:, cols].astype(jnp.float32) + r_ref[:, cols].astype(jnp.float32)
            out[cols, :] = jnp.transpose(total.astype(jnp.bfloat16))
        last = slot == len(SHIFTS) - 1
        results = refs[-2:] if slot and not last else refs[-1:]
        sent = results[0]
        own = pltpu.make_async_copy(out, sent, sem.at[0])
        if slot == 0:
            own.start()
        else:
            moved = slot_distance(meta_ref, slot) == SHIFTS[slot]
            pl.when(moved)(own.start)
            pl.when(jnp.logical_not(moved))(pltpu.make_async_copy(before, sent, sem.at[0]).start)
        if slot and not last:
            copy = pltpu.make_async_copy(out, results[1], sem.at[1])
            copy.start()
            copy.wait()
        if last:
            dest = whole.at[pl.ds(first, width), pl.ds(piece_at(meta_ref, 0), PIECE)]
            stay = pltpu.make_async_copy(out, dest, sem.at[2])
            pl.when(jnp.logical_not(moved))(stay.start)
            pl.when(jnp.logical_not(moved))(stay.wait)
        own.wait()
    for exists, store in stores:
        pl.when(exists)(store.wait)


def finish(meta, slot, first, pair, before, arrivals, whole, target, token, cost):
    last = slot == len(SHIFTS) - 1
    into = bool(arrivals) or last
    arrays = list(pair) + ([before] if slot else []) + [chunk for _, _, chunk in arrivals]
    specs = [pl.BlockSpec(array.shape, lambda g, meta: (0, 0)) for array in arrays]
    if token is not whole:
        arrays, specs = arrays + [token], specs + [ANY]
    aliases = {}
    scratch_shape = (pair[0].shape[1], PIECE) if pair else (16, HD)
    shapes = []
    if slot is not None:
        shapes = [jax.ShapeDtypeStruct(scratch_shape, jnp.bfloat16)] * (2 if slot and not last else 1)
    if into:
        if whole is not None:
            aliases = {1 + len(arrays): len(shapes)}
            arrays, specs = arrays + [whole], specs + [ANY]
        shapes.append(target)
    result = pl.pallas_call(
        functools.partial(finish_kernel, slot, first, into, [a[:2] for a in arrivals]),
        grid_spec=pltpu.PrefetchScalarGridSpec(
            num_scalar_prefetch=1,
            grid=(1,),
            in_specs=specs,
            out_specs=[ANY] * len(shapes),
            scratch_shapes=[
                pltpu.VMEM(scratch_shape, jnp.bfloat16), pltpu.SemaphoreType.DMA((3 + len(arrivals),))
            ],
        ),
        out_shape=shapes,
        input_output_aliases=aliases,
        compiler_params=params(),
        cost_estimate=cost,
    )(meta, *arrays)
    sent = result[0] if slot is not None else None
    return sent, result[1] if slot and not last else sent, result[-1] if into else whole


SHORT = pl.CostEstimate(flops=1000, bytes_accessed=1000, transcendentals=0)
LONG = pl.CostEstimate(flops=5 * 10**10, bytes_accessed=1000, transcendentals=0)

SHIFTS = (2, 3, 1)
CHUNKS = ((0, 0, 768), (0, 768, 512), (1, 0, 768), (1, 768, 512), (2, 0, 768), (2, 768, 512))
SHARES = ((0, (0, 1)), (1, (2, 3)), (2, (4, 5)))
CUT = None
STEPS = (
    "s0", "o1", "o0", "f1", "s1", "p1", "s2", "f0", "o4", "p0", "o3", "o2", "f3", "o5", "f2", "p3", "f4",
    "p2", "f5", "p4", "p5",
)
COUNT_LONG = ("f0", "f1", "f3", "f4", "o0", "o1", "o4", "s0",)


def pipeline(meta, queries, keys, values, segment, w_out, w_scale):
    groups = lax.axis_size("dp")
    ranks = lax.axis_size("tensor")
    features = w_out.shape[1] // ranks
    other_core = [(i, i ^ 1) for i in range(ranks)]
    other_chip = [(i, i ^ 2) for i in range(ranks)]
    target = jax.ShapeDtypeStruct((features, queries.shape[0]), jnp.bfloat16)
    inputs = (queries, keys, values, segment)
    attended, from_core, kept, from_chip, finished, arrived = {}, {}, {}, {}, {}, {}
    token, whole, waiting = meta, None, []
    finishes = sum(step[0] == "f" for step in STEPS)

    for step in STEPS:
        kind, index = step[0], int(step[1:])
        cost = LONG if step in COUNT_LONG else SHORT
        if kind == "s":
            slot, members = SHARES[index]
            ranges = [CHUNKS[i][1:] for i in members]
            parts, attended[slot] = sibling_part(
                meta, slot, ranges, CUT, inputs, attended.get(slot), w_out, w_scale, features, token, cost
            )
            token = parts[0][0]
            for i, arrays in zip(members, parts):
                from_core[i] = [lax.ppermute(array, "tensor", other_core) for array in arrays]
            continue
        slot, first, width = CHUNKS[index]
        if kind == "o":
            send, kept[index] = own_part(
                meta, (first, width), attended[slot], w_out, w_scale, from_core[index], features, token, cost
            )
            token = kept[index]
            from_chip[index] = lax.ppermute(send, "tensor", other_chip)
            continue
        if kind == "p":
            waiting.append((SHIFTS[slot], first, arrived[index]))
            if finishes:
                continue
            _, _, whole = finish(meta, None, first, (), None, waiting, whole, target, token, cost)
            token, waiting = whole, []
            continue
        finishes -= 1
        pair, before = (kept[index], from_chip[index]), finished.get((slot - 1, first))
        token, finished[slot, first], whole = finish(
            meta, slot, first, pair, before, waiting, whole, target, token, cost
        )
        waiting = []
        arrived[index] = lax.ppermute(token, "dp", [(i, (i + SHIFTS[slot]) % groups) for i in range(groups)])
    return whole


def attention_kernel(heads, q_ref, k_ref, v_ref, seg_ref, o_ref):
    attend_heads(heads, q_ref, k_ref, v_ref, segment_bias(seg_ref[0]), o_ref)


def attend_all(queries, keys, values, segment):
    rows, width = queries.shape
    heads = HEADS_STEP if (width // HD) % HEADS_STEP == 0 else 1
    block = pl.BlockSpec((PIECE, heads * HD), lambda i, g: (i, g))
    return pl.pallas_call(
        functools.partial(attention_kernel, heads),
        grid=(rows // PIECE, width // (heads * HD)),
        in_specs=[block, block, block, pl.BlockSpec((1, 1, PIECE), lambda i, g: (i, 0, 0))],
        out_specs=block,
        out_shape=jax.ShapeDtypeStruct((rows, width), jnp.bfloat16),
        compiler_params=params(),
    )(queries, keys, values, segment)


def general(queries, keys, values, segment, w_out, w_scale, handover):
    row_count, width = queries.shape
    piece_count = handover.shape[0]
    groups, my_group = lax.axis_size("dp"), lax.axis_index("dp")
    attended = attend_all(queries, keys, values, segment.reshape(-1, 1, PIECE))
    scale_rows, scale_cols = w_scale.shape
    blocked = w_out.astype(jnp.float32).reshape(scale_rows, HD, scale_cols, w_out.shape[1] // scale_cols)
    weight = (blocked * w_scale[:, None, :, None]).reshape(w_out.shape).astype(jnp.bfloat16)
    partial = lax.dot_general(weight, attended, (((0,), (1,)), ((), ())), preferred_element_type=jnp.float32)
    home = lax.psum_scatter(partial.astype(jnp.bfloat16), "tensor", scatter_dimension=0, tiled=True)
    pieces = home.reshape(home.shape[0], piece_count, PIECE)
    slots = jnp.arange(groups, dtype=jnp.int32)
    goes = (jnp.mod(my_group + handover, groups)[None, :] == slots[:, None]).astype(jnp.bfloat16)
    comes = (jnp.mod(my_group - handover, groups)[:, None] == slots[None, :]).astype(jnp.bfloat16)
    outgoing = jnp.einsum("tj,cjp->tcp", goes, pieces, preferred_element_type=jnp.float32).astype(jnp.bfloat16)
    arrived = lax.all_to_all(outgoing, "dp", split_axis=0, concat_axis=0, tiled=True)
    handed = jnp.einsum("jt,tcp->cjp", comes, arrived, preferred_element_type=jnp.float32).astype(jnp.bfloat16)
    return handed.reshape(home.shape[0], row_count)


def local(queries, keys, values, segment, w_out, w_scale, handover):
    fits = (
        lax.axis_size("dp") == 4
        and lax.axis_size("tensor") == 4
        and handover.shape[0] == 3
        and w_out.shape == (1536, 4 * 1280)
        and queries.shape[0] == 3 * PIECE
    )
    if not fits:
        return general(queries, keys, values, segment, w_out, w_scale, handover)
    meta = jnp.concatenate([lax.axis_index("tensor").astype(jnp.int32)[None], handover])
    return pipeline(meta, queries, keys, values, segment.reshape(-1, 1, PIECE), w_out, w_scale)


def solution(mesh):
    return jax.shard_map(
        local,
        mesh=mesh,
        in_specs=(
            P(("parts", "dp"), "tensor"),
            P(("parts", "dp"), "tensor"),
            P(("parts", "dp"), "tensor"),
            P(("parts", "dp")),
            P("tensor", None),
            P("tensor", None),
            P("parts"),
        ),
        out_specs=P("tensor", ("parts", "dp")),
        check_vma=False,
    )
```
